256 devices in a mesh: seq: 64 (over z_hi, x, y, core), tp: 4 (over z_lo).
Axes of the slice: x: 4, y: 4, z: 8 (z_hi: 2, z_lo: 4; z = z_hi * 4 + z_lo), core: 2. Of those that a mesh axis runs over, the one named last changes fastest.
Arguments:
- cotangent: bfloat16 [49152, 2048], P('seq', 'tp'), may hold values from -16 to 16
- gate_codes: bfloat16 [49152, 7168], P('seq', 'tp'), may hold values from -127 to 127, as said below
- up_codes: bfloat16 [49152, 7168], P('seq', 'tp'), may hold values from -127 to 127, as said below
- gate_scale: float32 [49152], P('seq'), may hold values from 0.004 to 0.04
- up_scale: float32 [49152], P('seq'), may hold values from 0.004 to 0.04
- down_weight: bfloat16 [2048, 7168], P('seq', 'tp'), may hold values from -0.125 to 0.125
Outputs:
- gate_grad: bfloat16 [49152, 7168], P('seq', 'tp')
- up_grad: bfloat16 [49152, 7168], P('seq', 'tp')
- weight_grad: float32 [2048, 7168], P('seq', 'tp')
The draws below stay inside these ranges and needn't reach their ends.
Inputs may be any that keep to these rules, and one draw needn't show every extreme that they name: `gate_codes`: every entry is a whole number. `up_codes`: every entry is a whole number.
All inputs are finite; a program needn't handle non-finite values.
Results may differ from the reference program's by a relative error of at most 0.003.
Values may be sent and summed in bfloat16 or wider, within the bound.
No kernel may reach another device: no remote copies, remote signals or barrier semaphores. Data moves between devices by JAX's collectives and lax.ppermute only.
A program may use at most 128 MiB of HBM per device.

```python
import math
import jax
import jax.numpy as jnp
from jax import lax

D = 2048
FF = 7168
TOKENS = 49152


def draw_gate_codes(key, part):
    key = jax.random.fold_in(key, 11)
    codes = jax.random.randint(key, (TOKENS, FF), -127, 128)
    return codes.astype(jnp.float32).astype(jnp.bfloat16)


def draw_up_codes(key, part):
    key = jax.random.fold_in(key, 23)
    codes = jax.random.randint(key, (TOKENS, FF), -127, 128)
    return codes.astype(jnp.float32).astype(jnp.bfloat16)


def raised(drawn, own_key, source, target, blocks, factor):
    owner, partner = [(jnp.arange(drawn.shape[dim]) // (drawn.shape[dim] // blocks)).reshape([-1 if axis == dim else 1 for axis in range(drawn.ndim)]) for dim in (source, target)]
    chosen = jax.random.permutation(own_key, blocks)[partner]
    strong = (owner == chosen) | (owner == (partner + blocks // 2) % blocks)
    return jnp.where(strong, factor * drawn, drawn)


def steps_of(key, extent, cuts, smallest, high):
    factor_of, own = 1.0, jax.random.fold_in(key, 6)
    for dim, parts in cuts:
        heights = jnp.exp(jax.random.uniform(jax.random.fold_in(own, dim), (parts,), jnp.float32, smallest / len(cuts), high / len(cuts)))
        factor_of = factor_of * jnp.repeat(heights, extent[dim] // parts).reshape([-1 if axis == dim else 1 for axis in range(len(extent))])
    return factor_of


def centred(rng, shape, width, limit, shards=(), kind=jnp.bfloat16):
    loudness = steps_of(rng, shape, shards, -0.22, 0.18) if shards else 1.0
    drawn = jax.random.normal(rng, shape, jnp.float32) * width * loudness
    return jnp.minimum(jnp.maximum(drawn, -limit), limit).astype(kind)


def bell_draw_with(rng, shape, scale, most, shards, heavy, kind=jnp.bfloat16):
    drawn = scale * jax.random.normal(rng, shape, jnp.float32)
    if shards:
        drawn = drawn * steps_of(rng, shape, shards, -0.22, 0.18)
    return jnp.clip(raised(drawn, jax.random.fold_in(rng, 3), *heavy), -most, most).astype(kind)


def setup_inputs(seed: int = 0) -> dict:
    key_of = jax.random.split(jax.random.key(seed), 7)
    return {
        "cotangent": bell_draw_with(key_of[0], (TOKENS, D), 1.0, 16.0, ((0, 64), (1, 4)), (0, 1, 64, 4.0)),
        "gate_codes": draw_gate_codes(jax.random.fold_in(key_of[6], 71), 0),
        "up_codes": draw_up_codes(jax.random.fold_in(key_of[6], 71), 0),
        "gate_scale": jnp.clip(jnp.exp(math.log(0.04) - 2.30258502 * jax.random.uniform(key_of[3], (TOKENS,), jnp.float32) ** steps_of(key_of[3], (TOKENS,), ((0, 64),), -0.2, 0.2)), 0.004, 0.04),
        "up_scale": jnp.clip(jnp.exp(math.log(0.04) - 2.30258502 * jax.random.uniform(key_of[4], (TOKENS,), jnp.float32) ** steps_of(key_of[4], (TOKENS,), ((0, 64),), -0.2, 0.2)), 0.004, 0.04),
        "down_weight": centred(key_of[5], (D, FF), D ** -0.5, 0.125, ((0, 64), (1, 4))),
    }


def reference(cotangent, gate_codes, up_codes, gate_scale, up_scale, down_weight):
    block_rows = math.gcd(TOKENS, 4096)
    block_count = TOKENS // block_rows
    normalizer = 1.0 / math.sqrt(TOKENS)

    def one_block(running, block_index):
        offset = (block_index * block_rows).astype(jnp.int32)
        cot_rows = lax.dynamic_slice_in_dim(cotangent, offset, block_rows, 0)
        gate_rows = lax.dynamic_slice_in_dim(gate_codes, offset, block_rows, 0)
        up_rows = lax.dynamic_slice_in_dim(up_codes, offset, block_rows, 0)
        gate_factor = lax.dynamic_slice_in_dim(gate_scale, offset, block_rows, 0)
        up_factor = lax.dynamic_slice_in_dim(up_scale, offset, block_rows, 0)
        gate_value = gate_rows.astype(jnp.float32) * gate_factor[:, None]
        up_value = up_rows.astype(jnp.float32) * up_factor[:, None]
        sigmoid_gate = jax.nn.sigmoid(gate_value)
        hidden_act = (gate_value * sigmoid_gate * up_value).astype(jnp.bfloat16)
        hidden_grad = jnp.dot(cot_rows, down_weight, preferred_element_type=jnp.float32)
        gate_out = (hidden_grad * up_value * sigmoid_gate * (1.0 + gate_value * (1.0 - sigmoid_gate))).astype(jnp.bfloat16)
        up_out = (hidden_grad * gate_value * sigmoid_gate).astype(jnp.bfloat16)
        running = running + lax.dot_general(cot_rows, hidden_act, (((0,), (0,)), ((), ())), preferred_element_type=jnp.float32)
        return (running, (gate_out, up_out))
    initial = jnp.zeros((D, FF), jnp.float32)
    indices = jnp.arange(block_count, dtype=jnp.int32)
    summed, outputs = lax.scan(one_block, initial, indices)
    gate_grad = outputs[0].reshape(TOKENS, FF)
    up_grad = outputs[1].reshape(TOKENS, FF)
    weight_grad = summed * normalizer
    return (gate_grad, up_grad, weight_grad)
```

```python
import math

import jax
import jax.numpy as jnp
from jax import lax
from jax.experimental import pallas as pl
from jax.experimental.pallas import tpu as pltpu
from jax.sharding import Mesh, PartitionSpec as P

SEQ = ("zh", "x", "y", "c")
BF, F32 = jnp.bfloat16, jnp.float32
BLOCK = 128
VMEM = 58 << 20


def shift(n, k):
    return [(i, (i + k) % n) for i in range(n)]


def flip(n, m):
    return [(i, i ^ m) for i in range(n)]


def after(value, *events):
    return lax.optimization_barrier((value, events))[0]


def cost(seconds):
    return pl.CostEstimate(flops=int(seconds * 1e15), bytes_accessed=0, transcendentals=0)


def column(row):
    return jnp.broadcast_to(row, (8, BLOCK)).T[:, :1]


def gates(gate_codes, up_codes, gate_scale, up_scale):
    g = gate_codes[...].astype(F32) * column(gate_scale[0])
    u = up_codes[...].astype(F32) * column(up_scale[0])
    return g, u, jax.nn.sigmoid(g)


def hidden_kernel(gate_codes, up_codes, gate_scale, up_scale, out):
    g, u, s = gates(gate_codes, up_codes, gate_scale, up_scale)
    out[...] = (g * s * u).astype(BF)


def hidden_of(gate_codes, up_codes, gate_scale, up_scale):
    tokens, cols = gate_codes.shape
    rows = pl.BlockSpec((BLOCK, cols), lambda i: (i, 0))
    scale = pl.BlockSpec((1, 1, BLOCK), lambda i: (i, 0, 0))
    return pl.pallas_call(
        hidden_kernel,
        grid=(tokens // BLOCK,),
        in_specs=[rows, rows, scale, scale],
        out_specs=rows,
        out_shape=jax.ShapeDtypeStruct((tokens, cols), BF),
        compiler_params=pltpu.CompilerParams(vmem_limit_bytes=VMEM),
        cost_estimate=cost(50e-6),
    )(gate_codes, up_codes, gate_scale, up_scale)


def grads_kernel(places, *refs):
    slots, others, weight = refs[:4], refs[4:8], refs[8]
    gate_codes, up_codes, gate_scale, up_scale = refs[9:13]
    gate_out, up_out, whole, sems = refs[-4:]

    def part(k, c):
        return pltpu.make_async_copy(weight.at[places[k], :, places[4 + c]], whole.at[k, c], sems.at[k, c])

    parts = [(k, c) for k in range(4) for c in range(2)]

    @pl.when(pl.program_id(0) == 0)
    def _():
        for k, c in parts:
            part(k, c).start()

    grad = None
    for k, c in parts:
        pl.when(pl.program_id(0) == 0)(part(k, c).wait)
        rows = (slots, others)[c][k][...].T
        term = jnp.dot(rows, whole[k, c].reshape(256, -1), preferred_element_type=F32)
        grad = term if grad is None else grad + term
    g, u, s = gates(gate_codes, up_codes, gate_scale, up_scale)
    gate_out[...] = (grad * u * s * (1.0 + g * (1.0 - s))).astype(BF)
    up_out[...] = (grad * g * s).astype(BF)


def grads_of(places, slots, others, weight, codes):
    tokens, cols = codes[0].shape
    rows = pl.BlockSpec((BLOCK, cols), lambda i, _: (i, 0))
    scale = pl.BlockSpec((1, 1, BLOCK), lambda i, _: (i, 0, 0))
    slot = pl.BlockSpec((256, BLOCK), lambda i, _: (0, i))
    out = jax.ShapeDtypeStruct((tokens, cols), BF)
    given = (places, *slots, *others, weight, *codes)
    return pl.pallas_call(
        grads_kernel,
        grid_spec=pltpu.PrefetchScalarGridSpec(
            num_scalar_prefetch=1,
            grid=(tokens // BLOCK,),
            in_specs=[slot] * 8
            + [pl.BlockSpec(memory_space=pltpu.HBM)]
            + [rows, rows, scale, scale],
            out_specs=[rows, rows],
            scratch_shapes=[pltpu.VMEM((4, 2, 8, 32, cols), BF), pltpu.SemaphoreType.DMA((4, 2))],
        ),
        out_shape=[out, out],
        compiler_params=pltpu.CompilerParams(vmem_limit_bytes=VMEM),
        cost_estimate=cost(50e-6),
    )(*given)


def owner_of_first(x, t):
    return (t - (t + x // 2) % 2) % 4 // 2


def on_device(cot, gate_codes, up_codes, gate_scale, up_scale, weight):
    zh, x, y, c, t = (lax.axis_index(n) for n in ("zh", "x", "y", "c", "t"))
    tokens, cols = gate_codes.shape
    normalizer = 1.0 / math.sqrt(tokens * 64)
    codes = (gate_codes, up_codes, gate_scale.reshape(-1, 1, BLOCK), up_scale.reshape(-1, 1, BLOCK))

    bar = lax.optimization_barrier

    def for_grads(slot):
        return over_core(slot[:, tokens:])

    def ring(slot):
        return lax.ppermute(slot, "t", shift(4, 1))

    def over_core(block):
        return lax.ppermute(block, "c", shift(2, 1))

    def over_y(near, far, opposite):
        return [lax.ppermute(b, "y", shift(4, d)) for d, b in ((1, near), (3, far), (2, opposite))]

    def summed(own, got):
        for block in got:
            own = own + block.astype(F32)
        return own

    def products(slot):
        total = jnp.dot(slot[:, :tokens], mine, preferred_element_type=F32)
        total += jnp.dot(slot[:, tokens:], other, preferred_element_type=F32)
        total = total.reshape(2, 4, 32, cols)
        block = lambda d: lax.dynamic_index_in_dim(total, (y + d) % 4, 1, keepdims=False)
        return block(0), block(1).astype(BF), block(3).astype(BF), block(2).astype(BF)

    def at_x(even, odd):
        def rows(m):
            to = x ^ m
            block = lambda a: lax.dynamic_index_in_dim(a, to % 2, 0, keepdims=False)
            return jnp.where(t % 2 == to // 2, block(even), block(odd))

        return rows

    def over_x(places, rows):
        return [lax.ppermute(rows(m).astype(BF), "x", flip(4, m)) for m in places]

    a = cot.T.reshape(2, 4, 2, 32, tokens).transpose(2, 0, 1, 3, 4).reshape(2, 256, tokens)
    kept, sent = lax.optimization_barrier((jnp.where(c == 0, a[0], a[1]), jnp.where(c == 0, a[1], a[0])))
    peer = lax.ppermute(after(weight, sent), "zh", shift(2, 1))
    mine = hidden_of(*codes)
    slot0, mine, peer = bar((jnp.concatenate([kept, over_core(sent)], axis=1), mine, peer))
    held = jnp.where(zh == 0, jnp.stack([weight, peer]), jnp.stack([peer, weight]))
    whole = lax.all_gather(held, ("x", "y", "c"), axis=1, tiled=True)

    slot1 = ring(slot0)
    other = over_core(mine)
    other0 = for_grads(slot0)
    p0 = products(slot0)
    slot1, other, other0, p0, slot0 = bar((slot1, other, other0, p0, slot0))

    slot2 = ring(slot1)
    y0 = over_y(*p0[1:])
    other1 = for_grads(slot1)
    p1 = products(slot1)
    slot2, y0, other1, p1, slot1 = bar((slot2, y0, other1, p1, slot1))

    slot3 = ring(slot2)
    y1 = over_y(*p1[1:])
    other2 = for_grads(slot2)
    p2 = products(slot2)
    slot3, y1, other2, p2, slot2 = bar((slot3, y1, other2, p2, slot2))

    y0, y1 = bar((summed(p0[0], y0), summed(p1[0], y1)))
    y2 = over_y(*p2[1:])
    x01 = over_x((1,), at_x(y0, y1))
    other3 = for_grads(slot3)
    p3 = products(slot3)
    y2, x01, p3, slot3, other3, whole = bar((y2, x01, p3, slot3, other3, whole))

    places = jnp.stack([(t - k) % 4 for k in range(4)] + [c, 1 - c]).astype(jnp.int32)
    slots = (slot0, slot1, slot2, slot3)
    others = (other0, other1, other2, other3)
    y3 = over_y(*p3[1:])
    x01 += over_x((3, 2), at_x(y0, y1))
    grads = grads_of(places, slots, others, whole.reshape(4, 8, 2, 32, cols), codes)
    y2 = summed(p2[0], y2)
    y2, y3, x01, grads = bar((y2, y3, x01, grads))

    y3 = summed(p3[0], y3)
    x23 = over_x((1, 3, 2), at_x(y2, y3))
    first = summed(at_x(y0, y1)(0), x01)
    x23, first = bar((x23, first))
    second = summed(at_x(y2, y3)(0), x23)

    here = owner_of_first(x, t) == zh
    got = lax.ppermute(jnp.where(here, second, first).astype(BF), "zh", shift(2, 1))
    weight_grad = (jnp.where(here, first, second) + got.astype(F32)) * normalizer
    return grads[0], grads[1], weight_grad


def solution(mesh):
    fine = Mesh(mesh.devices.reshape(2, 4, 4, 2, 4), SEQ + ("t",))
    both, rows = P(SEQ, "t"), P(SEQ)
    return jax.shard_map(
        on_device,
        mesh=fine,
        in_specs=(both, both, both, rows, rows, both),
        out_specs=(both, both, both),
        check_vma=False,
    )
```

```python
import math

import jax
import jax.numpy as jnp
from jax import lax
from jax.experimental import pallas as pl
from jax.experimental.pallas import tpu as pltpu
from jax.sharding import Mesh, PartitionSpec as P

SEQ = ("zh", "x", "y", "c")
BF, F32 = jnp.bfloat16, jnp.float32
BLOCK = 128
WIDE = 256
VMEM = 58 << 20


def shift(n, k):
    return [(i, (i + k) % n) for i in range(n)]


def flip(n, m):
    return [(i, i ^ m) for i in range(n)]


def after(value, *events):
    return lax.optimization_barrier((value, events))[0]


def cost(seconds):
    return pl.CostEstimate(flops=int(seconds * 1e15), bytes_accessed=0, transcendentals=0)


def column(row):
    return jnp.broadcast_to(row, (8, BLOCK)).T[:, :1]


def hidden_kernel(gate_codes, up_codes, gate_scale, up_scale, out):
    for i in range(gate_scale.shape[0]):
        rows = slice(i * BLOCK, (i + 1) * BLOCK)
        g = gate_codes[rows, :].astype(F32) * column(gate_scale[i])
        u = up_codes[rows, :].astype(F32) * column(up_scale[i])
        out[rows, :] = (g * jax.nn.sigmoid(g) * u).astype(BF)


def hidden_of(gate_codes, up_codes, gate_scale, up_scale):
    tokens, cols = gate_codes.shape
    rows = pl.BlockSpec((tokens // 2, cols), lambda i: (i, 0))
    scale = pl.BlockSpec((tokens // 2 // BLOCK, 1, BLOCK), lambda i: (i, 0, 0))
    return pl.pallas_call(
        hidden_kernel,
        grid=(2,),
        in_specs=[rows, rows, scale, scale],
        out_specs=rows,
        out_shape=jax.ShapeDtypeStruct((tokens, cols), BF),
        compiler_params=pltpu.CompilerParams(vmem_limit_bytes=VMEM),
        cost_estimate=cost(50e-6),
    )(gate_codes, up_codes, gate_scale, up_scale)


def grads_kernel(places, *refs):
    slots, others, weight = refs[:4], refs[4:8], refs[8]
    gate_codes, up_codes, gate_scale, up_scale = refs[9:13]
    gate_out, up_out, rows, scales = refs[-4:]
    tokens = gate_out.shape[0]

    @pl.when(pl.program_id(0) == 0)
    def _():
        for k in range(4):
            rows[k, 0] = slots[k][...].T
            rows[k, 1] = others[k][...].T
        for i in range(tokens // BLOCK):
            for j, scale in enumerate((gate_scale, up_scale)):
                scales[j, i * BLOCK : (i + 1) * BLOCK, :] = column(scale[i])

    grad = None
    for k in range(4):
        for c in range(2):
            part = weight[places[k], :, places[4 + c]].reshape(256, -1)
            term = jnp.dot(rows[k, c], part, preferred_element_type=F32)
            grad = term if grad is None else grad + term
    g = gate_codes[...].astype(F32) * scales[0]
    u = up_codes[...].astype(F32) * scales[1]
    s = jax.nn.sigmoid(g)
    gate_out[...] = (grad * u * s * (1.0 + g * (1.0 - s))).astype(BF)
    up_out[...] = (grad * g * s).astype(BF)


def grads_of(places, slots, others, weight, codes):
    tokens, cols = codes[0].shape
    block = pl.BlockSpec((tokens, WIDE), lambda i, _: (0, i))
    once = lambda *shape: pl.BlockSpec(shape, lambda i, _: (0,) * len(shape), pipeline_mode=pl.Buffered(1))
    out = jax.ShapeDtypeStruct((tokens, cols), BF)
    return pl.pallas_call(
        grads_kernel,
        grid_spec=pltpu.PrefetchScalarGridSpec(
            num_scalar_prefetch=1,
            grid=(cols // WIDE,),
            in_specs=[once(256, tokens)] * 8
            + [pl.BlockSpec((4, 8, 2, 32, WIDE), lambda i, _: (0, 0, 0, 0, i))]
            + [block, block]
            + [once(*a.shape) for a in codes[2:]],
            out_specs=[block, block],
            scratch_shapes=[pltpu.VMEM((4, 2, tokens, 256), BF), pltpu.VMEM((2, tokens, 1), F32)],
        ),
        out_shape=[out, out],
        compiler_params=pltpu.CompilerParams(vmem_limit_bytes=VMEM),
        cost_estimate=cost(50e-6),
    )(places, *slots, *others, weight, *codes)


def owner_of_first(x, t):
    return (t - (t + x // 2) % 2) % 4 // 2


def on_device(cot, gate_codes, up_codes, gate_scale, up_scale, weight):
    zh, x, y, c, t = (lax.axis_index(n) for n in ("zh", "x", "y", "c", "t"))
    tokens, cols = gate_codes.shape
    normalizer = 1.0 / math.sqrt(tokens * 64)
    codes = (gate_codes, up_codes, gate_scale.reshape(-1, 1, BLOCK), up_scale.reshape(-1, 1, BLOCK))

    bar = lax.optimization_barrier

    def for_grads(slot):
        return over_core(slot[:, tokens:])

    def ring(slot):
        return lax.ppermute(slot, "t", shift(4, 1))

    def over_core(block):
        return lax.ppermute(block, "c", shift(2, 1))

    def over_y(near, far, opposite):
        return [lax.ppermute(b, "y", shift(4, d)) for d, b in ((1, near), (3, far), (2, opposite))]

    def summed(own, got):
        for block in got:
            own = own + block.astype(F32)
        return own

    def products(slot):
        total = jnp.dot(slot[:, :tokens], mine, preferred_element_type=F32)
        total += jnp.dot(slot[:, tokens:], other, preferred_element_type=F32)
        total = total.reshape(2, 4, 32, cols)
        block = lambda d: lax.dynamic_index_in_dim(total, (y + d) % 4, 1, keepdims=False)
        return block(0), block(1).astype(BF), block(3).astype(BF), block(2).astype(BF)

    def at_x(even, odd):
        def rows(m):
            to = x ^ m
            block = lambda a: lax.dynamic_index_in_dim(a, to % 2, 0, keepdims=False)
            return jnp.where(t % 2 == to // 2, block(even), block(odd))

        return rows

    def over_x(places, rows):
        return [lax.ppermute(rows(m).astype(BF), "x", flip(4, m)) for m in places]

    a = cot.T.reshape(2, 4, 2, 32, tokens).transpose(2, 0, 1, 3, 4).reshape(2, 256, tokens)
    kept, sent = lax.optimization_barrier((jnp.where(c == 0, a[0], a[1]), jnp.where(c == 0, a[1], a[0])))
    peer = lax.ppermute(after(weight, sent), "zh", shift(2, 1))
    mine = hidden_of(*codes)
    slot0, mine, peer = bar((jnp.concatenate([kept, over_core(sent)], axis=1), mine, peer))
    held = jnp.where(zh == 0, jnp.stack([weight, peer]), jnp.stack([peer, weight]))
    whole = lax.all_gather(held, ("x", "y", "c"), axis=1, tiled=True)

    slot1 = ring(slot0)
    other = over_core(mine)
    other0 = for_grads(slot0)
    p0 = products(slot0)
    slot1, other, other0, p0, slot0 = bar((slot1, other, other0, p0, slot0))

    slot2 = ring(slot1)
    y0 = over_y(*p0[1:])
    other1 = for_grads(slot1)
    p1 = products(slot1)
    slot2, y0, other1, p1, slot1 = bar((slot2, y0, other1, p1, slot1))

    slot3 = ring(slot2)
    y1 = over_y(*p1[1:])
    other2 = for_grads(slot2)
    p2 = products(slot2)
    slot3, y1, other2, p2, slot2 = bar((slot3, y1, other2, p2, slot2))

    y0, y1 = bar((summed(p0[0], y0), summed(p1[0], y1)))
    y2 = over_y(*p2[1:])
    x01 = over_x((1,), at_x(y0, y1))
    other3 = for_grads(slot3)
    p3 = products(slot3)
    y2, x01, p3, slot3, other3, whole, tt, cc = bar((y2, x01, p3, slot3, other3, whole, t, c))

    places = jnp.stack([(tt - k) % 4 for k in range(4)] + [cc, 1 - cc]).astype(jnp.int32)
    slots = (slot0, slot1, slot2, slot3)
    others = (other0, other1, other2, other3)
    y3 = over_y(*p3[1:])
    x01 += over_x((3, 2), at_x(y0, y1))
    grads = grads_of(places, slots, others, whole.reshape(4, 8, 2, 32, cols), codes)
    y2 = summed(p2[0], y2)
    y2, y3, x01, grads = bar((y2, y3, x01, grads))

    y3 = summed(p3[0], y3)
    x23 = over_x((1, 3, 2), at_x(y2, y3))
    first = summed(at_x(y0, y1)(0), x01)
    x23, first = bar((x23, first))
    second = summed(at_x(y2, y3)(0), x23)

    here = owner_of_first(x, t) == zh
    got = lax.ppermute(jnp.where(here, second, first).astype(BF), "zh", shift(2, 1))
    weight_grad = (jnp.where(here, first, second) + got.astype(F32)) * normalizer
    return grads[0], grads[1], weight_grad


def solution(mesh):
    fine = Mesh(mesh.devices.reshape(2, 4, 4, 2, 4), SEQ + ("t",))
    both, rows = P(SEQ, "t"), P(SEQ)
    return jax.shard_map(
        on_device,
        mesh=fine,
        in_specs=(both, both, both, rows, rows, both),
        out_specs=(both, both, both),
        check_vma=False,
    )
```

```python
import math

import jax
import jax.numpy as jnp
from jax import lax
from jax.experimental import pallas as pl
from jax.experimental.pallas import tpu as pltpu
from jax.sharding import Mesh, PartitionSpec as P

SEQ = ("zh", "x", "y", "c")
BF, F32 = jnp.bfloat16, jnp.float32
BLOCK = 128
WIDE = 256
VMEM = 58 << 20


def shift(n, k):
    return [(i, (i + k) % n) for i in range(n)]


def flip(n, m):
    return [(i, i ^ m) for i in range(n)]


def after(value, *events):
    return lax.optimization_barrier((value, events))[0]


def cost(seconds):
    return pl.CostEstimate(flops=int(seconds * 1e15), bytes_accessed=0, transcendentals=0)


def column(scale, at):
    row = scale[pl.ds(at, BLOCK)].reshape(1, BLOCK)
    return jnp.broadcast_to(row, (8, BLOCK)).T[:, :1]


def hidden_kernel(gate_codes, up_codes, gate_scale, up_scale, out):
    tokens = out.shape[0]
    for i in range(0, tokens, BLOCK):
        rows = slice(i, i + BLOCK)
        at = pl.multiple_of(pl.program_id(0) * tokens + i, BLOCK)
        g = gate_codes[rows, :].astype(F32) * column(gate_scale, at)
        u = up_codes[rows, :].astype(F32) * column(up_scale, at)
        out[rows, :] = (g * jax.nn.sigmoid(g) * u).astype(BF)


def hidden_of(gate_codes, up_codes, gate_scale, up_scale):
    tokens, cols = gate_codes.shape
    rows = pl.BlockSpec((tokens // 2, cols), lambda i: (i, 0))
    scale = pl.BlockSpec((tokens,), lambda i: (0,))
    return pl.pallas_call(
        hidden_kernel,
        grid=(2,),
        in_specs=[rows, rows, scale, scale],
        out_specs=rows,
        out_shape=jax.ShapeDtypeStruct((tokens, cols), BF),
        compiler_params=pltpu.CompilerParams(vmem_limit_bytes=VMEM),
        cost_estimate=cost(50e-6),
    )(gate_codes, up_codes, gate_scale, up_scale)


def grads_kernel(places, *refs):
    slots, others, weight = refs[:4], refs[4:8], refs[8]
    gate_codes, up_codes, gate_scale, up_scale = refs[9:13]
    gate_out, up_out, rows, scales = refs[-4:]
    tokens = gate_out.shape[0]

    @pl.when(pl.program_id(0) == 0)
    def _():
        for k in range(4):
            rows[k, 0] = slots[k][...].T
            rows[k, 1] = others[k][...].T
        for i in range(tokens // BLOCK):
            for j, scale in enumerate((gate_scale, up_scale)):
                scales[j, i * BLOCK : (i + 1) * BLOCK, :] = column(scale, i * BLOCK)

    grad = None
    for k in range(4):
        for c in range(2):
            part = weight[places[k], :, places[4 + c]].reshape(256, -1)
            term = jnp.dot(rows[k, c], part, preferred_element_type=F32)
            grad = term if grad is None else grad + term
    g = gate_codes[...].astype(F32) * scales[0]
    u = up_codes[...].astype(F32) * scales[1]
    s = jax.nn.sigmoid(g)
    gate_out[...] = (grad * u * s * (1.0 + g * (1.0 - s))).astype(BF)
    up_out[...] = (grad * g * s).astype(BF)


def grads_of(places, slots, others, weight, codes):
    tokens, cols = codes[0].shape
    block = pl.BlockSpec((tokens, WIDE), lambda i, _: (0, i))
    once = lambda *shape: pl.BlockSpec(shape, lambda i, _: (0,) * len(shape), pipeline_mode=pl.Buffered(1))
    out = jax.ShapeDtypeStruct((tokens, cols), BF)
    return pl.pallas_call(
        grads_kernel,
        grid_spec=pltpu.PrefetchScalarGridSpec(
            num_scalar_prefetch=1,
            grid=(cols // WIDE,),
            in_specs=[once(256, tokens)] * 8
            + [pl.BlockSpec((4, 8, 2, 32, WIDE), lambda i, _: (0, 0, 0, 0, i))]
            + [block, block]
            + [once(*a.shape) for a in codes[2:]],
            out_specs=[block, block],
            scratch_shapes=[pltpu.VMEM((4, 2, tokens, 256), BF), pltpu.VMEM((2, tokens, 1), F32)],
        ),
        out_shape=[out, out],
        compiler_params=pltpu.CompilerParams(vmem_limit_bytes=VMEM),
        cost_estimate=cost(50e-6),
    )(places, *slots, *others, weight, *codes)


def owner_of_first(x, t):
    return (t - (t + x // 2) % 2) % 4 // 2


def on_device(cot, gate_codes, up_codes, gate_scale, up_scale, weight):
    zh, x, y, c, t = (lax.axis_index(n) for n in ("zh", "x", "y", "c", "t"))
    tokens, cols = gate_codes.shape
    normalizer = 1.0 / math.sqrt(tokens * 64)
    codes = (gate_codes, up_codes, gate_scale, up_scale)

    bar = lax.optimization_barrier

    def for_grads(slot):
        return over_core(slot[:, tokens:])

    def ring(slot):
        return lax.ppermute(slot, "t", shift(4, 1))

    def over_core(block):
        return lax.ppermute(block, "c", shift(2, 1))

    def over_y(near, far, opposite):
        return [lax.ppermute(b, "y", shift(4, d)) for d, b in ((1, near), (3, far), (2, opposite))]

    def summed(own, got):
        for block in got:
            own = own + block.astype(F32)
        return own

    def products(slot):
        total = jnp.dot(slot[:, :tokens], mine, preferred_element_type=F32)
        total += jnp.dot(slot[:, tokens:], other, preferred_element_type=F32)
        total = total.reshape(2, 4, 32, cols)
        block = lambda d: lax.dynamic_index_in_dim(total, (y + d) % 4, 1, keepdims=False)
        return block(0), block(1).astype(BF), block(3).astype(BF), block(2).astype(BF)

    def at_x(even, odd):
        def rows(m):
            to = x ^ m
            block = lambda a: lax.dynamic_index_in_dim(a, to % 2, 0, keepdims=False)
            return jnp.where(t % 2 == to // 2, block(even), block(odd))

        return rows

    def over_x(places, rows):
        return [lax.ppermute(rows(m).astype(BF), "x", flip(4, m)) for m in places]

    a = cot.T.reshape(2, 4, 2, 32, tokens).transpose(2, 0, 1, 3, 4).reshape(2, 256, tokens)
    kept, sent = lax.optimization_barrier((jnp.where(c == 0, a[0], a[1]), jnp.where(c == 0, a[1], a[0])))
    peer = lax.ppermute(after(weight, sent), "zh", shift(2, 1))
    mine = hidden_of(*codes)
    slot0, mine, peer = bar((jnp.concatenate([kept, over_core(sent)], axis=1), mine, peer))
    held = jnp.where(zh == 0, jnp.stack([weight, peer]), jnp.stack([peer, weight]))
    whole = lax.all_gather(held, ("x", "y", "c"), axis=1, tiled=True)

    slot1 = ring(slot0)
    other = over_core(mine)
    other0 = for_grads(slot0)
    p0 = products(slot0)
    slot1, other, other0, p0, slot0 = bar((slot1, other, other0, p0, slot0))

    slot2 = ring(slot1)
    y0 = over_y(*p0[1:])
    other1 = for_grads(slot1)
    p1 = products(slot1)
    slot2, y0, other1, p1, slot1 = bar((slot2, y0, other1, p1, slot1))

    slot3 = ring(slot2)
    y1 = over_y(*p1[1:])
    other2 = for_grads(slot2)
    p2 = products(slot2)
    slot3, y1, other2, p2, slot2 = bar((slot3, y1, other2, p2, slot2))

    y0, y1 = bar((summed(p0[0], y0), summed(p1[0], y1)))
    y2 = over_y(*p2[1:])
    x01 = over_x((1,), at_x(y0, y1))
    other3 = for_grads(slot3)
    p3 = products(slot3)
    y2, x01, p3, slot3, other3, whole, tt, cc = bar((y2, x01, p3, slot3, other3, whole, t, c))

    places = jnp.stack([(tt - k) % 4 for k in range(4)] + [cc, 1 - cc]).astype(jnp.int32)
    slots = (slot0, slot1, slot2, slot3)
    others = (other0, other1, other2, other3)
    y3 = over_y(*p3[1:])
    x01 += over_x((3, 2), at_x(y0, y1))
    grads = grads_of(places, slots, others, whole.reshape(4, 8, 2, 32, cols), codes)
    y2 = summed(p2[0], y2)
    y2, y3, x01, grads = bar((y2, y3, x01, grads))

    y3 = summed(p3[0], y3)
    x23 = over_x((1, 3, 2), at_x(y2, y3))
    first = summed(at_x(y0, y1)(0), x01)
    x23, first = bar((x23, first))
    second = summed(at_x(y2, y3)(0), x23)

    here = owner_of_first(x, t) == zh
    got = lax.ppermute(jnp.where(here, second, first).astype(BF), "zh", shift(2, 1))
    weight_grad = (jnp.where(here, first, second) + got.astype(F32)) * normalizer
    return grads[0], grads[1], weight_grad


def solution(mesh):
    fine = Mesh(mesh.devices.reshape(2, 4, 4, 2, 4), SEQ + ("t",))
    both, rows = P(SEQ, "t"), P(SEQ)
    return jax.shard_map(
        on_device,
        mesh=fine,
        in_specs=(both, both, both, rows, rows, both),
        out_specs=(both, both, both),
        check_vma=False,
    )
```

```python
import math

import jax
import jax.numpy as jnp
from jax import lax
from jax.experimental import pallas as pl
from jax.experimental.pallas import tpu as pltpu
from jax.sharding import Mesh, PartitionSpec as P

SEQ = ("zh", "x", "y", "c")
BF, F32 = jnp.bfloat16, jnp.float32
BLOCK = 128
WIDE = 256
VMEM = 58 << 20


def shift(n, k):
    return [(i, (i + k) % n) for i in range(n)]


def flip(n, m):
    return [(i, i ^ m) for i in range(n)]


def after(value, *events):
    return lax.optimization_barrier((value, events))[0]


def cost(seconds):
    return pl.CostEstimate(flops=int(seconds * 1e15), bytes_accessed=0, transcendentals=0)


def column(scale, at):
    row = scale[pl.ds(at, BLOCK)].reshape(1, BLOCK)
    return jnp.broadcast_to(row, (8, BLOCK)).T[:, :1]


def hidden_kernel(gate_codes, up_codes, gate_scale, up_scale, out):
    tokens = out.shape[0]
    for i in range(0, tokens, BLOCK):
        rows = slice(i, i + BLOCK)
        at = pl.multiple_of(pl.program_id(0) * tokens + i, BLOCK)
        g = gate_codes[rows, :].astype(F32) * column(gate_scale, at)
        u = up_codes[rows, :].astype(F32) * column(up_scale, at)
        out[rows, :] = (g * jax.nn.sigmoid(g) * u).astype(BF)


def hidden_of(gate_codes, up_codes, gate_scale, up_scale):
    tokens, cols = gate_codes.shape
    rows = pl.BlockSpec((tokens // 2, cols), lambda i: (i, 0))
    scale = pl.BlockSpec((tokens,), lambda i: (0,))
    return pl.pallas_call(
        hidden_kernel,
        grid=(2,),
        in_specs=[rows, rows, scale, scale],
        out_specs=rows,
        out_shape=jax.ShapeDtypeStruct((tokens, cols), BF),
        compiler_params=pltpu.CompilerParams(vmem_limit_bytes=VMEM),
        cost_estimate=cost(50e-6),
    )(gate_codes, up_codes, gate_scale, up_scale)


def grads_kernel(places, *refs):
    slots, others, weight = refs[:4], refs[4:8], refs[8]
    gate_codes, up_codes, gate_scale, up_scale = refs[9:13]
    gate_out, up_out, rows, scales = refs[-4:]
    tokens = gate_out.shape[0]

    @pl.when(pl.program_id(0) == 0)
    def _():
        for k in range(4):
            rows[k, 0] = slots[k][...].T
            rows[k, 1] = others[k][...].T
        for i in range(tokens // BLOCK):
            for j, scale in enumerate((gate_scale, up_scale)):
                scales[j, i * BLOCK : (i + 1) * BLOCK, :] = column(scale, i * BLOCK)

    grad = None
    for k in range(4):
        for c in range(2):
            part = weight[places[k], :, places[4 + c]].reshape(256, -1)
            term = jnp.dot(rows[k, c], part, preferred_element_type=F32)
            grad = term if grad is None else grad + term
    g = gate_codes[...].astype(F32) * scales[0]
    u = up_codes[...].astype(F32) * scales[1]
    s = jax.nn.sigmoid(g)
    gate_out[...] = (grad * u * s * (1.0 + g * (1.0 - s))).astype(BF)
    up_out[...] = (grad * g * s).astype(BF)


def grads_of(places, slots, others, weight, codes):
    tokens, cols = codes[0].shape
    block = pl.BlockSpec((tokens, WIDE), lambda i, _: (0, i))
    once = lambda *shape: pl.BlockSpec(shape, lambda i, _: (0,) * len(shape), pipeline_mode=pl.Buffered(1))
    out = jax.ShapeDtypeStruct((tokens, cols), BF)
    return pl.pallas_call(
        grads_kernel,
        grid_spec=pltpu.PrefetchScalarGridSpec(
            num_scalar_prefetch=1,
            grid=(cols // WIDE,),
            in_specs=[once(256, tokens)] * 8
            + [pl.BlockSpec((4, 8, 2, 32, WIDE), lambda i, _: (0, 0, 0, 0, i))]
            + [block, block]
            + [once(*a.shape) for a in codes[2:]],
            out_specs=[block, block],
            scratch_shapes=[pltpu.VMEM((4, 2, tokens, 256), BF), pltpu.VMEM((2, tokens, 1), F32)],
        ),
        out_shape=[out, out],
        compiler_params=pltpu.CompilerParams(vmem_limit_bytes=VMEM),
        cost_estimate=cost(50e-6),
    )(places, *slots, *others, weight, *codes)


def owner_of_first(x, t):
    return (t - (t + x // 2) % 2) % 4 // 2


def on_device(cot, gate_codes, up_codes, gate_scale, up_scale, weight):
    zh, x, y, c, t = (lax.axis_index(n) for n in ("zh", "x", "y", "c", "t"))
    tokens, cols = gate_codes.shape
    normalizer = 1.0 / math.sqrt(tokens * 64)
    codes = (gate_codes, up_codes, gate_scale, up_scale)

    bar = lax.optimization_barrier

    def for_grads(slot):
        return over_core(slot[:, tokens:])

    def ring(slot):
        return lax.ppermute(slot, "t", shift(4, 1))

    def over_core(block):
        return lax.ppermute(block, "c", shift(2, 1))

    def over_y(near, far, opposite):
        return [lax.ppermute(b, "y", shift(4, d)) for d, b in ((1, near), (3, far), (2, opposite))]

    def summed(own, got):
        for block in got:
            own = own + block.astype(F32)
        return own

    def products(slot):
        total = jnp.dot(slot[:, :tokens], mine, preferred_element_type=F32)
        total += jnp.dot(slot[:, tokens:], other, preferred_element_type=F32)
        total = total.reshape(2, 4, 32, cols)
        block = lambda d: lax.dynamic_index_in_dim(total, (y + d) % 4, 1, keepdims=False)
        return block(0), block(1).astype(BF), block(3).astype(BF), block(2).astype(BF)

    def at_x(even, odd):
        def rows(m):
            to = x ^ m
            block = lambda a: lax.dynamic_index_in_dim(a, to % 2, 0, keepdims=False)
            return jnp.where(t % 2 == to // 2, block(even), block(odd))

        return rows

    def over_x(places, rows):
        return [lax.ppermute(rows(m).astype(BF), "x", flip(4, m)) for m in places]

    a = cot.T.reshape(2, 4, 2, 32, tokens).transpose(2, 0, 1, 3, 4).reshape(2, 256, tokens)
    kept, sent = lax.optimization_barrier((jnp.where(c == 0, a[0], a[1]), jnp.where(c == 0, a[1], a[0])))
    peer = lax.ppermute(after(weight, sent), "zh", shift(2, 1))
    mine = hidden_of(*codes)
    slot0, mine, peer = bar((jnp.concatenate([kept, over_core(sent)], axis=1), mine, peer))
    held = jnp.where(zh == 0, jnp.stack([weight, peer]), jnp.stack([peer, weight]))
    whole = lax.all_gather(held, ("x", "y", "c"), axis=1, tiled=True)

    slot1 = ring(slot0)
    other = over_core(mine)
    other0 = for_grads(slot0)
    p0 = products(slot0)
    slot1, other, other0, p0, slot0 = bar((slot1, other, other0, p0, slot0))

    slot2 = ring(slot1)
    y0 = over_y(*p0[1:])
    other1 = for_grads(slot1)
    p1 = products(slot1)
    slot2, y0, other1, p1, slot1 = bar((slot2, y0, other1, p1, slot1))

    slot3 = ring(slot2)
    y1 = over_y(*p1[1:])
    other2 = for_grads(slot2)
    p2 = products(slot2)
    slot3, y1, other2, p2, slot2 = bar((slot3, y1, other2, p2, slot2))

    y0, y1 = bar((summed(p0[0], y0), summed(p1[0], y1)))
    x01 = over_x((1,), at_x(y0, y1))
    other3 = for_grads(slot3)
    p3 = products(slot3)
    sent = [jnp.concatenate(blocks) for blocks in zip(p2[1:], p3[1:])]
    x01, sent, p3, slot3, other3, whole, tt, cc = bar((x01, sent, p3[0], slot3, other3, whole, t, c))

    places = jnp.stack([(tt - k) % 4 for k in range(4)] + [cc, 1 - cc]).astype(jnp.int32)
    slots = (slot0, slot1, slot2, slot3)
    others = (other0, other1, other2, other3)
    y23 = over_y(*sent)
    x01 += over_x((3, 2), at_x(y0, y1))
    grads = grads_of(places, slots, others, whole.reshape(4, 8, 2, 32, cols), codes)
    y23, x01, grads = bar((y23, x01, grads))

    y2 = summed(p2[0], [block[:2] for block in y23])
    y3 = summed(p3, [block[2:] for block in y23])
    x23 = over_x((1, 3, 2), at_x(y2, y3))
    first = summed(at_x(y0, y1)(0), x01)
    x23, first = bar((x23, first))
    second = summed(at_x(y2, y3)(0), x23)

    here = owner_of_first(x, t) == zh
    got = lax.ppermute(jnp.where(here, second, first).astype(BF), "zh", shift(2, 1))
    weight_grad = (jnp.where(here, first, second) + got.astype(F32)) * normalizer
    return grads[0], grads[1], weight_grad


def solution(mesh):
    fine = Mesh(mesh.devices.reshape(2, 4, 4, 2, 4), SEQ + ("t",))
    both, rows = P(SEQ, "t"), P(SEQ)
    return jax.shard_map(
        on_device,
        mesh=fine,
        in_specs=(both, both, both, rows, rows, both),
        out_specs=(both, both, both),
        check_vma=False,
    )
```
